32 devices in a mesh: grp: 2 (over y), gx: 4 (over z), gy: 2 (over x), gz: 2 (over core).
Axes of the slice: x: 2, y: 2, z: 4, core: 2. Of those that a mesh axis runs over, the one named last changes fastest.
Arguments:
- density: float32 [32, 256, 256], P(('grp', 'gz'), 'gx', 'gy'), parts along dimension 0, may hold values from -6 to 6
- sigma: float32 [32, 256, 256], P(('grp', 'gz'), 'gx', 'gy'), parts along dimension 0, may hold values from -6 to 6
- mt_values: bfloat16 [16, 8, 2, 16, 128], P(('grp', 'gx', 'gy'), None, None, 'gz'), parts along dimension 0, may hold values from -6 to 6
- mt_rows: int32 [16, 8, 2], P(('grp', 'gx', 'gy')), parts along dimension 0, may hold values from 0 to 63
- mt_counts: int32 [16, 8], P(('grp', 'gx', 'gy')), parts along dimension 0, may hold values from 0 to 2, as said below
- kernel: bfloat16 [6, 16, 17, 17], P(None, 'gz'), may hold values from -0.09375 to 0.09375
- observed: float32 [12, 256, 256], P('grp', 'gx', 'gy'), parts along dimension 0, may hold values from -6 to 6
Outputs:
- sigma_trial: float32 [32, 256, 256], P(('grp', 'gz'), 'gx', 'gy'), parts along dimension 0
- density_trial: float32 [32, 256, 256], P(('grp', 'gz'), 'gx', 'gy'), parts along dimension 0
- tensor_residual: float32 [12, 256, 256], P('grp', 'gx', 'gy'), parts along dimension 0
The draws below stay inside these ranges and needn't reach their ends.
There are 2 independent parts, one for each index of `grp`. The reference program is written for one: setup_inputs(seed, part) draws one part's arguments, and reference() takes and returns one part's arrays. A program takes and returns all parts, laid end to end along the dimension named above; an argument that names none is the same for every part. Nothing has to cross between parts.
Inputs may be any that keep to these rules, and one draw needn't show every extreme that they name: `mt_counts`: some owner tile receives 2 used slots from every source tile.
All inputs are finite; a program needn't handle non-finite values.
Results may differ from the reference program's by a relative error of at most 0.002.
Values may be sent and summed in bfloat16 or wider, within the bound.
A program may use at most 64 MiB of HBM per device.

```python
import jax
import jax.numpy as jnp
from jax import lax

CX = 64
CY = 128
CAP = 2
COMP = 6
KSIZE = 17
TILES = 8
NX = 256
NY = 256
NZ = 16
N_GX = 4
N_GY = 2


def draw_mt_counts(key, part):
    key = jax.random.fold_in(key, 11)
    first, second, third = jax.random.split(key, 3)
    owners = jnp.arange(TILES, dtype=jnp.int32)
    loaded = jax.random.randint(first, (TILES,), 0, 4) == 0
    chosen = jax.random.randint(second, (), 0, TILES)
    loaded = loaded | (owners == chosen)
    drawn = jax.random.randint(third, (TILES, TILES), 0, CAP)
    return jnp.where(loaded[None, :], CAP, drawn).astype(jnp.int32)


def with_ends(array, own_key, smallest, high):
    dims = array.shape
    index_at = [jax.random.randint(jax.random.fold_in(own_key, axis), (), 0, dims[axis]) for axis in range(len(dims))]
    array = array.at[tuple(index_at)].set(smallest)
    longest = dims.index(max(dims))
    index_at[longest] = (index_at[longest] + 1) % dims[longest]
    return array.at[tuple(index_at)].set(high)


def levels(rng, shape, cuts, least, top_value):
    level, own = 1.0, jax.random.fold_in(rng, 6)
    for position, parts in cuts:
        steps = jnp.exp(jax.random.uniform(jax.random.fold_in(own, position), (parts,), jnp.float32, least / len(cuts), top_value / len(cuts)))
        level = level * jnp.repeat(steps, shape[position] // parts).reshape([-1 if axis == position else 1 for axis in range(len(shape))])
    return level


def normal_values(own_key, dims, deviation, most, pieces=(), kind=jnp.bfloat16):
    values = jax.random.normal(own_key, dims, jnp.float32) * deviation
    if len(pieces) > 0:
        values = levels(own_key, dims, pieces, -0.22, 0.18) * values
    return jnp.clip(values, min=-most, max=most).astype(kind)


def setup_inputs(seed: int = 0, part: int = 0) -> dict:
    streams_of = jax.random.split(jax.random.key(seed), 8)
    own_keys = jax.random.split(jax.random.fold_in(streams_of[7], part), 8)
    density = normal_values(own_keys[0], (NZ, NX, NY), 1.0, 6.0, ((0, 2), (1, 4), (2, 2)), jnp.float32)
    sigma = normal_values(own_keys[1], (NZ, NX, NY), 1.0, 6.0, ((0, 2), (1, 4), (2, 2)), jnp.float32)
    mt_values = normal_values(own_keys[2], (TILES, TILES, CAP, NZ, CY), 1.0, 6.0, ((0, 8), (3, 2)))
    mt_rows = with_ends(jax.random.randint(own_keys[3], (TILES, TILES, CAP), 0, CX), jax.random.fold_in(own_keys[3], 1), 0, CX - 1).astype(jnp.int32)
    mt_counts = draw_mt_counts(jax.random.fold_in(jax.random.fold_in(streams_of[7], part), 71), part)
    kernel = normal_values(streams_of[5], (COMP, NZ, KSIZE, KSIZE), (NZ * KSIZE * KSIZE) ** -0.5, 0.09375, ((1, 2),))
    observed = normal_values(own_keys[6], (COMP, NX, NY), 1.0, 6.0, ((1, 4), (2, 2)), jnp.float32)
    return {"density": density, "sigma": sigma, "mt_values": mt_values, "mt_rows": mt_rows, "mt_counts": mt_counts, "kernel": kernel, "observed": observed}


step_sigma = 0.5
step_density = 0.25


def central(padded):
    along_x = (padded[1:-1, 2:, 1:-1] - padded[1:-1, :-2, 1:-1]) * 0.5
    along_y = (padded[1:-1, 1:-1, 2:] - padded[1:-1, 1:-1, :-2]) * 0.5
    along_z = (padded[2:, 1:-1, 1:-1] - padded[:-2, 1:-1, 1:-1]) * 0.5
    return (along_x, along_y, along_z)


def crossed(first, second):
    return (first[1] * second[2] - first[2] * second[1],
            first[2] * second[0] - first[0] * second[2],
            first[0] * second[1] - first[1] * second[0])


def divergence(padded):
    part_x = padded[0, 1:-1, 2:, 1:-1] - padded[0, 1:-1, :-2, 1:-1]
    part_y = padded[1, 1:-1, 1:-1, 2:] - padded[1, 1:-1, 1:-1, :-2]
    part_z = padded[2, 2:, 1:-1, 1:-1] - padded[2, :-2, 1:-1, 1:-1]
    return (part_x + part_y + part_z) * 0.5


def reference(density, sigma, mt_values, mt_rows, mt_counts, kernel, observed):
    slots = jnp.arange(CAP, dtype=jnp.int32)
    live = slots[None, None, :] < mt_counts[:, :, None]
    picks = ((mt_rows[..., None] == jnp.arange(CX, dtype=jnp.int32)) & live[..., None]).astype(jnp.float32)
    gathered = jnp.einsum("sdkr,sdkzy->dzry", picks, mt_values.astype(jnp.float32),
                          precision=lax.Precision.HIGHEST)
    grad_sum = gathered.reshape(N_GX, N_GY, NZ, CX, CY).transpose(2, 0, 3, 1, 4).reshape(NZ, NX, NY)
    sigma_trial = sigma - step_sigma * grad_sum
    grad_model = central(jnp.pad(density, 1))
    grad_cond = central(jnp.pad(sigma_trial, 1))
    cross_field = crossed(grad_model, grad_cond)
    flux = jnp.stack(crossed(grad_cond, cross_field))
    coupling = -2.0 * divergence(jnp.pad(flux, ((0, 0), (1, 1), (1, 1), (1, 1))))
    density_trial = density - step_density * coupling
    rounded = lax.optimization_barrier(density_trial.astype(jnp.bfloat16)).astype(jnp.float32)
    predicted = lax.conv_general_dilated(rounded[None], kernel.astype(jnp.float32), (1, 1),
                                         ((8, 8), (8, 8)), dimension_numbers=("NCHW", "OIHW", "NCHW"),
                                         precision=lax.Precision.HIGHEST)[0]
    return sigma_trial, density_trial, predicted - observed
```

```python
import functools

import jax
import jax.numpy as jnp
from jax import lax
from jax.experimental import pallas as pl
from jax.experimental.pallas import tpu as pltpu
from jax.sharding import PartitionSpec as P

MESH = pl.DeviceIdType.MESH
STEPS = ((-1, 0), (1, 0), (0, -1), (0, 1), (-1, -1), (-1, 1), (1, -1), (1, 1))
EDGE = 8


def packed_columns(layers, half):
    lane = lax.broadcasted_iota(jnp.int32, layers[0].shape, 1)
    result = jnp.zeros_like(layers[0])
    for i, layer in enumerate(layers):
        result = jnp.where(lane // (2 * half) == i, pltpu.roll(layer, half + 2 * half * i, 1), result)
    return result


def halo_columns(left, right, i, half):
    lane = lax.broadcasted_iota(jnp.int32, left.shape, 1)
    own = 2 * half * i
    return jnp.where(
        lane < 64,
        pltpu.roll(right, (128 - own - half) % 128, 1),
        pltpu.roll(left, (128 - half - own) % 128, 1),
    )


def body(
    sizes, density_ref, sigma_ref, payload_ref, taps_ref, observed_ref,
    sigma_out, density_out, residual_out,
    arrived, wide_d, wide_s, pack, sides, flux_z, lateral, rounded, toeplitz, blocks, part, other,
    all_send, all_recv, z_send, z_recv, near_send, near_recv, sum_send, sum_recv,
):
    n_gx, n_gy, n_gz = sizes
    tiles = n_gx * n_gy
    nz, rows, cols = density_ref.shape
    comps = observed_ref.shape[0]
    span = taps_ref.shape[0] // comps
    ext = rows + 2 * EDGE
    ix, iy, iz = lax.axis_index("gx"), lax.axis_index("gy"), lax.axis_index("gz")
    me = ix * n_gy + iy
    inner = pl.ds(EDGE, rows)
    own = pl.ds(0, cols)

    def over_tiles(step):
        if tiles <= 16:
            for off in range(1, tiles):
                step(off)
        else:
            lax.fori_loop(1, tiles, lambda off, _: (step(off), 0)[1], 0)

    for wide in (wide_d, wide_s):
        wide[...] = jnp.zeros_like(wide)
    sides[...] = jnp.zeros_like(sides)
    rounded[...] = jnp.zeros_like(rounded)

    barrier = pltpu.get_barrier_semaphore()

    def greet(off):
        tile = lax.rem(me + off, tiles)
        pl.semaphore_signal(
            barrier, inc=1, device_id={"gx": tile // n_gy, "gy": lax.rem(tile, n_gy)}, device_id_type=MESH
        )

    over_tiles(greet)
    for off in range(1, n_gz):
        pl.semaphore_signal(barrier, inc=1, device_id={"gz": lax.rem(iz + off, n_gz)}, device_id_type=MESH)
    pl.semaphore_wait(barrier, tiles - 1 + n_gz - 1)

    def block_copy(tile, source):
        return pltpu.make_async_remote_copy(
            src_ref=payload_ref.at[tile], dst_ref=arrived.at[source],
            send_sem=all_send.at[tile], recv_sem=all_recv.at[source],
            device_id={"gx": tile // n_gy, "gy": lax.rem(tile, n_gy)}, device_id_type=MESH,
        )

    over_tiles(lambda off: block_copy(lax.rem(me + off, tiles), me).start())
    arrived[me] = payload_ref[me]

    def z_copy(wide, field, up):
        src, dst = (pl.ds(nz, 2), pl.ds(0, 2)) if up else (pl.ds(2, 2), pl.ds(nz + 2, 2))
        return pltpu.make_async_remote_copy(
            src_ref=wide.at[src, inner, own], dst_ref=wide.at[dst, inner, own],
            send_sem=z_send.at[field, int(up)], recv_sem=z_recv.at[field, int(up)],
            device_id={"gz": lax.rem(iz + (1 if up else n_gz - 1), n_gz)}, device_id_type=MESH,
        )

    has_up, has_down = iz < n_gz - 1, iz > 0

    def z_start(wide, field):
        pl.when(has_up)(lambda: z_copy(wide, field, True).start())
        pl.when(has_down)(lambda: z_copy(wide, field, False).start())

    def z_finish(wide, field):
        @pl.when(has_up)
        def _():
            z_copy(wide, field, True).wait_send()
            z_copy(wide, field, False).wait_recv()

        @pl.when(has_down)
        def _():
            z_copy(wide, field, False).wait_send()
            z_copy(wide, field, True).wait_recv()

    def inside(x, y):
        return (x >= 0) & (x < n_gx) & (y >= 0) & (y < n_gy)

    def near_copy(wide, field, at, dx, dy, x, y):
        if dy == 0:
            src = wide.at[:, pl.ds(EDGE if dx < 0 else rows, EDGE), own]
            dst = wide.at[:, pl.ds(EDGE + rows if dx < 0 else 0, EDGE), own]
        else:
            side = 0 if dy > 0 else 1
            source, target, count = {
                0: (0, EDGE, rows), -1: (0, EDGE + rows, EDGE), 1: (rows - EDGE, 0, EDGE)
            }[dx]
            src = pack.at[field, pl.ds(source, count)]
            dst = sides.at[field, side, pl.ds(target, count)]
        return pltpu.make_async_remote_copy(
            src_ref=src, dst_ref=dst, send_sem=near_send.at[field, at], recv_sem=near_recv.at[field, at],
            device_id={"gx": x, "gy": y}, device_id_type=MESH,
        )

    def near_start(wide, field):
        for at, (dx, dy) in enumerate(STEPS):
            @pl.when(inside(ix + dx, iy + dy))
            def _():
                near_copy(wide, field, at, dx, dy, ix + dx, iy + dy).start()

    def near_finish(wide, field):
        for at, (dx, dy) in enumerate(STEPS):
            @pl.when(inside(ix - dx, iy - dy))
            def _():
                near_copy(wide, field, at, dx, dy, ix - dx, iy - dy).wait_recv()

            @pl.when(inside(ix + dx, iy + dy))
            def _():
                near_copy(wide, field, at, dx, dy, ix + dx, iy + dy).wait_send()

    def unpack(wide, field):
        for i in range(nz + 4):
            wide[i, :, pl.ds(cols, cols)] = halo_columns(sides[field, 0], sides[field, 1], i, 4)

    wide_d[pl.ds(2, nz), inner, own] = density_ref[...]
    z_start(wide_d, 0)

    depth = taps_ref.shape[1]
    for row in range(span * comps):
        for half in range(depth // 128):
            taps = jnp.broadcast_to(taps_ref[row : row + 1, half * 128 : (half + 1) * 128], (16, 128))
            band = pltpu.roll(taps, 0, 1, stride=1, stride_axis=0)
            toeplitz[row * 16 : (row + 1) * 16, half * 128 : (half + 1) * 128] = band.astype(jnp.bfloat16)

    z_finish(wide_d, 0)
    pack[0] = packed_columns([wide_d[i, inner, own] for i in range(nz + 4)], 4)
    near_start(wide_d, 0)

    def landed(off):
        tile = lax.rem(me + off, tiles)
        copy = block_copy(tile, tile)
        copy.wait_recv()

    over_tiles(landed)
    slots = tiles * 16
    values = arrived[:, 0:16, :].reshape(slots, cols)
    picks = arrived[:, 16:32, :].reshape(slots, 128).astype(jnp.float32).T
    slot_z = lax.rem(lax.broadcasted_iota(jnp.int32, (128, slots), 1), nz)
    row_z = lax.broadcasted_iota(jnp.int32, (128, slots), 0) // rows
    for g in range(nz // 2):
        chosen = jnp.where(slot_z == row_z + 2 * g, picks, 0.0).astype(jnp.bfloat16)
        total = jnp.dot(chosen, values, preferred_element_type=jnp.float32)
        for j in range(2):
            trial = sigma_ref[2 * g + j] - 0.5 * total[j * rows : (j + 1) * rows]
            wide_s[2 * g + j + 2, inner, own] = trial
            sigma_out[2 * g + j] = trial
    z_start(wide_s, 1)
    near_finish(wide_d, 0)
    unpack(wide_d, 0)
    z_finish(wide_s, 1)
    pack[1] = packed_columns([wide_s[i, inner, own] for i in range(nz + 4)], 4)
    near_start(wide_s, 1)
    near_finish(wide_s, 1)
    unpack(wide_s, 1)

    at_row = lax.broadcasted_iota(jnp.int32, (ext, 2 * cols), 0)
    at_lane = lax.broadcasted_iota(jnp.int32, (ext, 2 * cols), 1)
    row_in = ((at_row >= EDGE) | (ix > 0)) & ((at_row < EDGE + rows) | (ix < n_gx - 1))
    lane_in = (at_lane < cols) | ((at_lane < cols + 64) & (iy < n_gy - 1)) | ((at_lane >= cols + 64) & (iy > 0))

    def shifted(value, axis):
        size = value.shape[axis]
        return pltpu.roll(value, size - 1, axis) - pltpu.roll(value, 1, axis)

    def layer(i, _):
        def gradient(wide):
            here = wide[i]
            return shifted(here, 0) * 0.5, shifted(here, 1) * 0.5, (wide[i + 1] - wide[i - 1]) * 0.5

        dx, dy, dz = gradient(wide_d)
        sx, sy, sz = gradient(wide_s)
        cx, cy, cz = dy * sz - dz * sy, dz * sx - dx * sz, dx * sy - dy * sx
        fx = jnp.where(row_in, sy * cz - sz * cy, 0.0)
        fy = jnp.where(lane_in, sz * cx - sx * cz, 0.0)
        fz = sx * cy - sy * cx
        z_in = ((i >= 2) | has_down) & ((i < nz + 2) | has_up)
        flux_z[i] = jnp.where(z_in, fz[EDGE : EDGE + rows, :cols], 0.0)
        lateral[i] = (shifted(fx, 0) + shifted(fy, 1))[EDGE : EDGE + rows, :cols]
        return 0

    lax.fori_loop(1, nz + 3, layer, 0)
    for i in range(nz):
        trial = density_ref[i] + 0.25 * (lateral[i + 2] + (flux_z[i + 3] - flux_z[i + 1]))
        density_out[i] = trial
        rounded[i, inner, own] = trial.astype(jnp.bfloat16).astype(jnp.float32)
    pack[2] = packed_columns([rounded[i, inner, own] for i in range(nz)], 8)
    near_start(rounded, 2)
    near_finish(rounded, 2)
    for i in range(nz):
        rounded[i, :, pl.ds(cols, cols)] = halo_columns(sides[2, 0], sides[2, 1], i, 8)

    for s in range(rows // 16):
        for i in range(nz):
            blocks[s, i * 32 : (i + 1) * 32, :] = rounded[i, s * 16 : s * 16 + 32, :].astype(jnp.bfloat16)

    def section(s, _):
        block = blocks[s]
        total = jnp.zeros((comps * 16, cols), jnp.float32)
        for b in range(span):
            one = jnp.dot(
                toeplitz[b * comps * 16 : (b + 1) * comps * 16, :], block, preferred_element_type=jnp.float32
            )
            total = total + pltpu.roll(one, (8 - b) % (2 * cols), 1)[:, :cols]
        for c in range(comps):
            part[c, pl.ds(pl.multiple_of(s * 16, 16), 16), :] = total[c * 16 : (c + 1) * 16]
        return 0

    lax.fori_loop(0, rows // 16, section, 0)

    if n_gz > 1:
        swap = pltpu.make_async_remote_copy(
            src_ref=part, dst_ref=other, send_sem=sum_send, recv_sem=sum_recv,
            device_id={"gz": n_gz - 1 - iz}, device_id_type=MESH,
        )
        swap.start()
        over_tiles(lambda off: block_copy(lax.rem(me + off, tiles), me).wait_send())
        swap.wait()
        residual_out[...] = part[...] + other[...] - observed_ref[...]
    else:
        over_tiles(lambda off: block_copy(lax.rem(me + off, tiles), me).wait_send())
        residual_out[...] = part[...] - observed_ref[...]


def local(sizes, density, sigma, mt_values, mt_rows, mt_counts, kernel, observed):
    nz, rows, cols = density.shape
    tiles, capacity = mt_values.shape[1:3]
    comps, span = kernel.shape[0], kernel.shape[2]
    ext = rows + 2 * EDGE
    live = jnp.arange(capacity, dtype=jnp.int32)[None, :] < mt_counts[0][:, None]
    target = jnp.where(live, mt_rows[0], -1)
    picks = target[:, :, None, None] == jnp.arange(128, dtype=jnp.int32) % rows
    picks = jnp.broadcast_to(picks, (tiles, capacity, nz, 128)).reshape(tiles, capacity * nz, 128)
    payload = jnp.concatenate(
        [mt_values[0].reshape(tiles, capacity * nz, cols), picks.astype(jnp.bfloat16)], axis=1
    )
    taps = jnp.pad(kernel.transpose(3, 0, 1, 2), ((0, 0), (0, 0), (0, 0), (0, 32 - span)))
    taps = taps.reshape(span * comps, nz * 32).astype(jnp.float32)
    vmem = pl.BlockSpec(memory_space=pltpu.VMEM)
    f32 = jnp.float32
    dma = pltpu.SemaphoreType.DMA
    return pl.pallas_call(
        functools.partial(body, sizes),
        out_shape=(
            jax.ShapeDtypeStruct(sigma.shape, f32),
            jax.ShapeDtypeStruct(density.shape, f32),
            jax.ShapeDtypeStruct(observed.shape, f32),
        ),
        in_specs=[vmem] * 5,
        out_specs=(vmem,) * 3,
        scratch_shapes=[
            pltpu.VMEM(payload.shape, jnp.bfloat16),
            pltpu.VMEM((nz + 4, ext, 2 * cols), f32),
            pltpu.VMEM((nz + 4, ext, 2 * cols), f32),
            pltpu.VMEM((3, rows, 128), f32),
            pltpu.VMEM((3, 2, ext, 128), f32),
            pltpu.VMEM((nz + 4, rows, cols), f32),
            pltpu.VMEM((nz + 4, rows, cols), f32),
            pltpu.VMEM((nz, ext, 2 * cols), f32),
            pltpu.VMEM((span * comps * 16, nz * 32), jnp.bfloat16),
            pltpu.VMEM((rows // 16, nz * 32, 2 * cols), jnp.bfloat16),
            pltpu.VMEM(observed.shape, f32),
            pltpu.VMEM(observed.shape, f32),
            dma((tiles,)), dma((tiles,)), dma((2, 2)), dma((2, 2)),
            dma((3, 8)), dma((3, 8)), dma, dma,
        ],
        compiler_params=pltpu.CompilerParams(
            collective_id=0, has_side_effects=True, vmem_limit_bytes=40 * 1024 * 1024
        ),
    )(density, sigma, payload, taps, observed)


def solution(mesh):
    field = P(("grp", "gz"), "gx", "gy")
    placed = (
        field,
        field,
        P(("grp", "gx", "gy"), None, None, "gz", None),
        P(("grp", "gx", "gy"), None, None),
        P(("grp", "gx", "gy"), None),
        P(None, "gz", None, None),
        P("grp", "gx", "gy"),
    )
    sizes = (mesh.shape["gx"], mesh.shape["gy"], mesh.shape["gz"])
    return jax.shard_map(
        functools.partial(local, sizes),
        mesh=mesh,
        in_specs=placed,
        out_specs=(field, field, P("grp", "gx", "gy")),
        check_vma=False,
    )
```

```python
import functools

import jax
import jax.numpy as jnp
from jax import lax
from jax.experimental import pallas as pl
from jax.experimental.pallas import tpu as pltpu
from jax.sharding import PartitionSpec as P

MESH = pl.DeviceIdType.MESH
STEPS = ((-1, 0), (1, 0), (0, -1), (0, 1), (-1, -1), (-1, 1), (1, -1), (1, 1))
EDGE = 8


def packed_columns(layers, half):
    lane = lax.broadcasted_iota(jnp.int32, layers[0].shape, 1)
    result = jnp.zeros_like(layers[0])
    for i, layer in enumerate(layers):
        result = jnp.where(lane // (2 * half) == i, pltpu.roll(layer, half + 2 * half * i, 1), result)
    return result


def halo_columns(left, right, i, half):
    lane = lax.broadcasted_iota(jnp.int32, left.shape, 1)
    own = 2 * half * i
    return jnp.where(
        lane < 64,
        pltpu.roll(right, (128 - own - half) % 128, 1),
        pltpu.roll(left, (128 - half - own) % 128, 1),
    )


def body(
    sizes, density_ref, sigma_ref, values_in, rows_in, counts_in, taps_in, observed_ref,
    sigma_out, density_out, residual_out,
    sigma_in, observed_in, values_ref, rows_ref, counts_ref, taps_ref, payload, arrived, wide_d, wide_s, pack, sides, flux_z, lateral, rounded, toeplitz, blocks, part, other,
    load_sem, all_send, all_recv, z_send, z_recv, near_send, near_recv, sum_send, sum_recv,
):
    n_gx, n_gy, n_gz = sizes
    tiles = n_gx * n_gy
    nz, rows, cols = density_ref.shape
    comps = observed_ref.shape[0]
    span = taps_ref.shape[1]
    ext = rows + 2 * EDGE
    ix, iy, iz = lax.axis_index("gx"), lax.axis_index("gy"), lax.axis_index("gz")
    me = ix * n_gy + iy
    inner = pl.ds(EDGE, rows)
    own = pl.ds(0, cols)

    def over_tiles(step):
        if tiles <= 16:
            for off in range(1, tiles):
                step(off)
        else:
            lax.fori_loop(1, tiles, lambda off, _: (step(off), 0)[1], 0)

    loads = [
        pltpu.make_async_copy(density_ref, wide_d.at[pl.ds(2, nz), inner, own], load_sem.at[0]),
        pltpu.make_async_copy(sigma_ref, sigma_in, load_sem.at[1]),
        pltpu.make_async_copy(observed_ref, observed_in, load_sem.at[2]),
        pltpu.make_async_copy(values_in, values_ref, load_sem.at[3]),
        pltpu.make_async_copy(rows_in, rows_ref, load_sem.at[4]),
        pltpu.make_async_copy(counts_in, counts_ref, load_sem.at[5]),
        pltpu.make_async_copy(taps_in, taps_ref, load_sem.at[6]),
    ]
    for load in loads[3:] + loads[:3]:
        load.start()
    for wide in (wide_d, wide_s, rounded):
        depth = wide.shape[0]
        for first in (0, EDGE + rows):
            wide[:, first : first + EDGE, :cols] = jnp.zeros((depth, EDGE, cols), jnp.float32)
    for wide in (wide_d, wide_s):
        for first in (0, nz + 2):
            wide[first : first + 2, inner, own] = jnp.zeros((2, rows, cols), jnp.float32)
    sides[...] = jnp.zeros_like(sides)

    barrier = pltpu.get_barrier_semaphore()

    def greet(off):
        tile = lax.rem(me + off, tiles)
        pl.semaphore_signal(
            barrier, inc=1, device_id={"gx": tile // n_gy, "gy": lax.rem(tile, n_gy)}, device_id_type=MESH
        )

    over_tiles(greet)
    for off in range(1, n_gz):
        pl.semaphore_signal(barrier, inc=1, device_id={"gz": lax.rem(iz + off, n_gz)}, device_id_type=MESH)

    slot_row = lax.rem(lax.broadcasted_iota(jnp.int32, (nz, 128), 1), rows)

    def load_blocks(tile):
        payload[tile, 0:16, :] = values_ref[tile]
        picked = []
        for k in range(16 // nz):
            target = jnp.where(k < counts_ref[0, tile], rows_ref[k, tile], -1)
            picked.append(jnp.where(slot_row == target, 1.0, 0.0))
        payload[tile, 16:32, :] = jnp.concatenate(picked, axis=0).astype(jnp.bfloat16)

    for load in loads[3:6]:
        load.wait()
    if tiles <= 16:
        for tile in range(tiles):
            load_blocks(tile)
    else:
        lax.fori_loop(0, tiles, lambda tile, _: (load_blocks(tile), 0)[1], 0)
    pl.semaphore_wait(barrier, tiles - 1 + n_gz - 1)

    def block_copy(tile, source):
        return pltpu.make_async_remote_copy(
            src_ref=payload.at[tile], dst_ref=arrived.at[source],
            send_sem=all_send.at[tile], recv_sem=all_recv.at[source],
            device_id={"gx": tile // n_gy, "gy": lax.rem(tile, n_gy)}, device_id_type=MESH,
        )

    over_tiles(lambda off: block_copy(lax.rem(me + off, tiles), me).start())
    arrived[me] = payload[me]

    def z_copy(wide, field, up):
        src, dst = (pl.ds(nz, 2), pl.ds(0, 2)) if up else (pl.ds(2, 2), pl.ds(nz + 2, 2))
        return pltpu.make_async_remote_copy(
            src_ref=wide.at[src, inner, own], dst_ref=wide.at[dst, inner, own],
            send_sem=z_send.at[field, int(up)], recv_sem=z_recv.at[field, int(up)],
            device_id={"gz": lax.rem(iz + (1 if up else n_gz - 1), n_gz)}, device_id_type=MESH,
        )

    has_up, has_down = iz < n_gz - 1, iz > 0

    def z_start(wide, field):
        pl.when(has_up)(lambda: z_copy(wide, field, True).start())
        pl.when(has_down)(lambda: z_copy(wide, field, False).start())

    def z_finish(wide, field):
        @pl.when(has_up)
        def _():
            z_copy(wide, field, True).wait_send()
            z_copy(wide, field, False).wait_recv()

        @pl.when(has_down)
        def _():
            z_copy(wide, field, False).wait_send()
            z_copy(wide, field, True).wait_recv()

    def inside(x, y):
        return (x >= 0) & (x < n_gx) & (y >= 0) & (y < n_gy)

    def near_copy(wide, field, at, dx, dy, x, y):
        if dy == 0:
            src = wide.at[:, pl.ds(EDGE if dx < 0 else rows, EDGE), own]
            dst = wide.at[:, pl.ds(EDGE + rows if dx < 0 else 0, EDGE), own]
        else:
            side = 0 if dy > 0 else 1
            source, target, count = {
                0: (0, EDGE, rows), -1: (0, EDGE + rows, EDGE), 1: (rows - EDGE, 0, EDGE)
            }[dx]
            src = pack.at[field, pl.ds(source, count)]
            dst = sides.at[field, side, pl.ds(target, count)]
        return pltpu.make_async_remote_copy(
            src_ref=src, dst_ref=dst, send_sem=near_send.at[field, at], recv_sem=near_recv.at[field, at],
            device_id={"gx": x, "gy": y}, device_id_type=MESH,
        )

    def near_start(wide, field, faces):
        for at, (dx, dy) in enumerate(STEPS):
            if (dy == 0) != faces:
                continue

            @pl.when(inside(ix + dx, iy + dy))
            def _():
                near_copy(wide, field, at, dx, dy, ix + dx, iy + dy).start()

    def near_finish(wide, field):
        for at, (dx, dy) in enumerate(STEPS):
            @pl.when(inside(ix - dx, iy - dy))
            def _():
                near_copy(wide, field, at, dx, dy, ix - dx, iy - dy).wait_recv()

            @pl.when(inside(ix + dx, iy + dy))
            def _():
                near_copy(wide, field, at, dx, dy, ix + dx, iy + dy).wait_send()

    def unpack(wide, field):
        for i in range(nz + 4):
            wide[i, :, pl.ds(cols, cols)] = halo_columns(sides[field, 0], sides[field, 1], i, 4)

    loads[0].wait()
    z_start(wide_d, 0)

    depth = nz * 32
    place_row = lax.broadcasted_iota(jnp.int32, (span * nz, depth), 0)
    place_lane = lax.broadcasted_iota(jnp.int32, (span * nz, depth), 1)
    place = place_lane == lax.rem(place_row, nz) * 32 + place_row // nz
    place = jnp.where(place, 1.0, 0.0).astype(jnp.bfloat16)
    loads[6].wait()
    for c in range(comps):
        footprint = taps_ref[c].astype(jnp.float32).reshape(span * nz, span).astype(jnp.bfloat16)
        lines = lax.dot_general(
            footprint, place, (((0,), (0,)), ((), ())), preferred_element_type=jnp.float32
        )
        for b in range(span):
            first = (b * comps + c) * 16
            for half in range(depth // 128):
                taps = jnp.broadcast_to(lines[b : b + 1, half * 128 : (half + 1) * 128], (16, 128))
                band = pltpu.roll(taps, 0, 1, stride=1, stride_axis=0)
                toeplitz[first : first + 16, half * 128 : (half + 1) * 128] = band.astype(jnp.bfloat16)

    z_finish(wide_d, 0)
    near_start(wide_d, 0, True)
    pack[0] = packed_columns([wide_d[i, inner, own] for i in range(nz + 4)], 4)
    near_start(wide_d, 0, False)

    def landed(off):
        tile = lax.rem(me + off, tiles)
        copy = block_copy(tile, tile)
        copy.wait_recv()

    loads[1].wait()
    over_tiles(landed)
    slots = tiles * 16
    values = arrived[:, 0:16, :].reshape(slots, cols)
    picks = arrived[:, 16:32, :].reshape(slots, 128).astype(jnp.float32).T
    slot_z = lax.rem(lax.broadcasted_iota(jnp.int32, (128, slots), 1), nz)
    row_z = lax.broadcasted_iota(jnp.int32, (128, slots), 0) // rows
    for g in range(nz // 2):
        chosen = jnp.where(slot_z == row_z + 2 * g, picks, 0.0).astype(jnp.bfloat16)
        total = jnp.dot(chosen, values, preferred_element_type=jnp.float32)
        for j in range(2):
            trial = sigma_in[2 * g + j] - 0.5 * total[j * rows : (j + 1) * rows]
            wide_s[2 * g + j + 2, inner, own] = trial
            sigma_out[2 * g + j] = trial
    z_start(wide_s, 1)
    near_finish(wide_d, 0)
    unpack(wide_d, 0)
    z_finish(wide_s, 1)
    near_start(wide_s, 1, True)
    pack[1] = packed_columns([wide_s[i, inner, own] for i in range(nz + 4)], 4)
    near_start(wide_s, 1, False)
    near_finish(wide_s, 1)
    unpack(wide_s, 1)

    at_row = lax.broadcasted_iota(jnp.int32, (ext, 2 * cols), 0)
    at_lane = lax.broadcasted_iota(jnp.int32, (ext, 2 * cols), 1)
    row_in = ((at_row >= EDGE) | (ix > 0)) & ((at_row < EDGE + rows) | (ix < n_gx - 1))
    lane_in = (at_lane < cols) | ((at_lane < cols + 64) & (iy < n_gy - 1)) | ((at_lane >= cols + 64) & (iy > 0))

    def shifted(value, axis):
        size = value.shape[axis]
        return pltpu.roll(value, size - 1, axis) - pltpu.roll(value, 1, axis)

    def layer(i, _):
        def gradient(wide):
            here = wide[i]
            return shifted(here, 0) * 0.5, shifted(here, 1) * 0.5, (wide[i + 1] - wide[i - 1]) * 0.5

        dx, dy, dz = gradient(wide_d)
        sx, sy, sz = gradient(wide_s)
        cx, cy, cz = dy * sz - dz * sy, dz * sx - dx * sz, dx * sy - dy * sx
        fx = jnp.where(row_in, sy * cz - sz * cy, 0.0)
        fy = jnp.where(lane_in, sz * cx - sx * cz, 0.0)
        fz = sx * cy - sy * cx
        z_in = ((i >= 2) | has_down) & ((i < nz + 2) | has_up)
        flux_z[i] = jnp.where(z_in, fz[EDGE : EDGE + rows, :cols], 0.0)
        lateral[i] = (shifted(fx, 0) + shifted(fy, 1))[EDGE : EDGE + rows, :cols]
        return 0

    lax.fori_loop(1, nz + 3, layer, 0)
    for i in range(nz):
        trial = wide_d[i + 2, inner, own] + 0.25 * (lateral[i + 2] + (flux_z[i + 3] - flux_z[i + 1]))
        density_out[i] = trial
        rounded[i, inner, own] = trial.astype(jnp.bfloat16).astype(jnp.float32)
    near_start(rounded, 2, True)
    pack[2] = packed_columns([rounded[i, inner, own] for i in range(nz)], 8)
    near_start(rounded, 2, False)
    near_finish(rounded, 2)
    for i in range(nz):
        rounded[i, :, pl.ds(cols, cols)] = halo_columns(sides[2, 0], sides[2, 1], i, 8)

    for s in range(rows // 16):
        for i in range(nz):
            blocks[s, i * 32 : (i + 1) * 32, :] = rounded[i, s * 16 : s * 16 + 32, :].astype(jnp.bfloat16)

    def swap(s):
        return pltpu.make_async_remote_copy(
            src_ref=part.at[:, pl.ds(s * 16, 16), :], dst_ref=other.at[:, pl.ds(s * 16, 16), :],
            send_sem=sum_send.at[s], recv_sem=sum_recv.at[s],
            device_id={"gz": n_gz - 1 - iz}, device_id_type=MESH,
        )

    for s in range(rows // 16):
        block = blocks[s]
        total = jnp.zeros((comps * 16, cols), jnp.float32)
        for b in range(span):
            one = jnp.dot(
                toeplitz[b * comps * 16 : (b + 1) * comps * 16, :], block, preferred_element_type=jnp.float32
            )
            total = total + pltpu.roll(one, (8 - b) % (2 * cols), 1)[:, :cols]
        for c in range(comps):
            part[c, s * 16 : (s + 1) * 16, :] = total[c * 16 : (c + 1) * 16]
        if n_gz > 1:
            swap(s).start()

    loads[2].wait()
    over_tiles(lambda off: block_copy(lax.rem(me + off, tiles), me).wait_send())
    for s in range(rows // 16):
        here = pl.ds(s * 16, 16)
        if n_gz > 1:
            swap(s).wait()
            residual_out[:, here, :] = part[:, here, :] + other[:, here, :] - observed_in[:, here, :]
        else:
            residual_out[:, here, :] = part[:, here, :] - observed_in[:, here, :]


def local(sizes, density, sigma, mt_values, mt_rows, mt_counts, kernel, observed):
    nz, rows, cols = density.shape
    tiles, capacity = mt_values.shape[1:3]
    comps, span = kernel.shape[0], kernel.shape[2]
    ext = rows + 2 * EDGE
    blocks = mt_values[0].reshape(tiles, capacity * nz, cols)
    taps = kernel.transpose(0, 2, 1, 3)
    vmem = pl.BlockSpec(memory_space=pltpu.VMEM)
    whole = pl.BlockSpec(memory_space=pltpu.HBM)
    f32 = jnp.float32
    dma = pltpu.SemaphoreType.DMA
    shapes = tuple(jax.ShapeDtypeStruct(like.shape, f32) for like in (sigma, density, observed))
    return pl.pallas_call(
        functools.partial(body, sizes),
        out_shape=shapes,
        in_specs=[whole] * 7,
        out_specs=(vmem,) * 3,
        scratch_shapes=[
            pltpu.VMEM(sigma.shape, f32),
            pltpu.VMEM(observed.shape, f32),
            pltpu.VMEM(blocks.shape, jnp.bfloat16),
            pltpu.SMEM((capacity, tiles), jnp.int32),
            pltpu.SMEM((1, tiles), jnp.int32),
            pltpu.VMEM(taps.shape, jnp.bfloat16),
            pltpu.VMEM((tiles, 32, 128), jnp.bfloat16),
            pltpu.VMEM((tiles, 32, 128), jnp.bfloat16),
            pltpu.VMEM((nz + 4, ext, 2 * cols), f32),
            pltpu.VMEM((nz + 4, ext, 2 * cols), f32),
            pltpu.VMEM((3, rows, 128), f32),
            pltpu.VMEM((3, 2, ext, 128), f32),
            pltpu.VMEM((nz + 4, rows, cols), f32),
            pltpu.VMEM((nz + 4, rows, cols), f32),
            pltpu.VMEM((nz, ext, 2 * cols), f32),
            pltpu.VMEM((span * comps * 16, nz * 32), jnp.bfloat16),
            pltpu.VMEM((rows // 16, nz * 32, 2 * cols), jnp.bfloat16),
            pltpu.VMEM(observed.shape, f32),
            pltpu.VMEM(observed.shape, f32),
            dma((7,)), dma((tiles,)), dma((tiles,)), dma((2, 2)), dma((2, 2)),
            dma((3, 8)), dma((3, 8)), dma((rows // 16,)), dma((rows // 16,)),
        ],
        compiler_params=pltpu.CompilerParams(
            collective_id=0, has_side_effects=True, vmem_limit_bytes=57 * 1024 * 1024
        ),
    )(density, sigma, blocks, mt_rows[0].T, mt_counts, taps, observed)


def solution(mesh):
    field = P(("grp", "gz"), "gx", "gy")
    placed = (
        field,
        field,
        P(("grp", "gx", "gy"), None, None, "gz", None),
        P(("grp", "gx", "gy"), None, None),
        P(("grp", "gx", "gy"), None),
        P(None, "gz", None, None),
        P("grp", "gx", "gy"),
    )
    sizes = (mesh.shape["gx"], mesh.shape["gy"], mesh.shape["gz"])
    return jax.shard_map(
        functools.partial(local, sizes),
        mesh=mesh,
        in_specs=placed,
        out_specs=(field, field, P("grp", "gx", "gy")),
        check_vma=False,
    )
```

```python
import functools

import jax
import jax.numpy as jnp
from jax import lax
from jax.experimental import pallas as pl
from jax.experimental.pallas import tpu as pltpu
from jax.sharding import PartitionSpec as P

MESH = pl.DeviceIdType.MESH
STEPS = ((-1, 0), (1, 0), (0, -1), (0, 1), (-1, -1), (-1, 1), (1, -1), (1, 1))
EDGE = 8


def packed_columns(layers, half):
    lane = lax.broadcasted_iota(jnp.int32, layers[0].shape, 1)
    result = jnp.zeros_like(layers[0])
    for i, layer in enumerate(layers):
        result = jnp.where(lane // (2 * half) == i, pltpu.roll(layer, half + 2 * half * i, 1), result)
    return result


def halo_columns(left, right, i, half):
    lane = lax.broadcasted_iota(jnp.int32, left.shape, 1)
    own = 2 * half * i
    return jnp.where(
        lane < 64,
        pltpu.roll(right, (128 - own - half) % 128, 1),
        pltpu.roll(left, (128 - half - own) % 128, 1),
    )


def body(
    sizes, density_ref, sigma_ref, values_in, rows_in, counts_in, taps_in, observed_ref,
    sigma_out, density_out, residual_out,
    sigma_in, observed_in, values_ref, rows_ref, counts_ref, taps_ref, payload, arrived, wide_d, wide_s, pack, sides, flux_z, lateral, rounded, toeplitz, blocks, part, other,
    load_sem, all_send, all_recv, z_send, z_recv, near_send, near_recv, sum_send, sum_recv,
):
    n_gx, n_gy, n_gz = sizes
    tiles = n_gx * n_gy
    nz, rows, cols = density_ref.shape
    comps = observed_ref.shape[0]
    span = taps_ref.shape[1]
    ext = rows + 2 * EDGE
    ix, iy, iz = lax.axis_index("gx"), lax.axis_index("gy"), lax.axis_index("gz")
    me = ix * n_gy + iy
    inner = pl.ds(EDGE, rows)
    own = pl.ds(0, cols)

    def over_tiles(step):
        if tiles <= 16:
            for off in range(1, tiles):
                step(off)
        else:
            lax.fori_loop(1, tiles, lambda off, _: (step(off), 0)[1], 0)

    loads = [
        pltpu.make_async_copy(density_ref, wide_d.at[pl.ds(2, nz), inner, own], load_sem.at[0]),
        pltpu.make_async_copy(sigma_ref, sigma_in, load_sem.at[1]),
        pltpu.make_async_copy(observed_ref, observed_in, load_sem.at[2]),
        pltpu.make_async_copy(values_in, values_ref, load_sem.at[3]),
        pltpu.make_async_copy(rows_in, rows_ref, load_sem.at[4]),
        pltpu.make_async_copy(counts_in, counts_ref, load_sem.at[5]),
        pltpu.make_async_copy(taps_in, taps_ref, load_sem.at[6]),
    ]
    for load in loads[3:] + loads[:3]:
        load.start()
    for wide in (wide_d, wide_s, rounded):
        depth = wide.shape[0]
        for first in (0, EDGE + rows):
            wide[:, first : first + EDGE, :cols] = jnp.zeros((depth, EDGE, cols), jnp.float32)
    for wide in (wide_d, wide_s):
        for first in (0, nz + 2):
            wide[first : first + 2, inner, own] = jnp.zeros((2, rows, cols), jnp.float32)
    sides[...] = jnp.zeros_like(sides)

    barrier = pltpu.get_barrier_semaphore()

    def greet(off):
        tile = lax.rem(me + off, tiles)
        pl.semaphore_signal(
            barrier, inc=1, device_id={"gx": tile // n_gy, "gy": lax.rem(tile, n_gy)}, device_id_type=MESH
        )

    over_tiles(greet)
    for off in range(1, n_gz):
        pl.semaphore_signal(barrier, inc=1, device_id={"gz": lax.rem(iz + off, n_gz)}, device_id_type=MESH)

    slot_row = lax.rem(lax.broadcasted_iota(jnp.int32, (nz, 128), 1), rows)

    def load_blocks(tile):
        payload[tile, 0:16, :] = values_ref[tile]
        picked = []
        for k in range(16 // nz):
            target = jnp.where(k < counts_ref[0, tile], rows_ref[k, tile], -1)
            picked.append(jnp.where(slot_row == target, 1.0, 0.0))
        payload[tile, 16:32, :] = jnp.concatenate(picked, axis=0).astype(jnp.bfloat16)

    for load in loads[3:6]:
        load.wait()
    if tiles <= 16:
        for tile in range(tiles):
            load_blocks(tile)
    else:
        lax.fori_loop(0, tiles, lambda tile, _: (load_blocks(tile), 0)[1], 0)
    pl.semaphore_wait(barrier, tiles - 1 + n_gz - 1)

    def block_copy(tile, source):
        return pltpu.make_async_remote_copy(
            src_ref=payload.at[tile], dst_ref=arrived.at[source],
            send_sem=all_send.at[tile], recv_sem=all_recv.at[source],
            device_id={"gx": tile // n_gy, "gy": lax.rem(tile, n_gy)}, device_id_type=MESH,
        )

    over_tiles(lambda off: block_copy(lax.rem(me + off, tiles), me).start())
    arrived[me] = payload[me]

    def z_copy(wide, field, up):
        src, dst = (pl.ds(nz, 2), pl.ds(0, 2)) if up else (pl.ds(2, 2), pl.ds(nz + 2, 2))
        return pltpu.make_async_remote_copy(
            src_ref=wide.at[src, inner, own], dst_ref=wide.at[dst, inner, own],
            send_sem=z_send.at[field, int(up)], recv_sem=z_recv.at[field, int(up)],
            device_id={"gz": lax.rem(iz + (1 if up else n_gz - 1), n_gz)}, device_id_type=MESH,
        )

    has_up, has_down = iz < n_gz - 1, iz > 0

    def z_start(wide, field):
        pl.when(has_up)(lambda: z_copy(wide, field, True).start())
        pl.when(has_down)(lambda: z_copy(wide, field, False).start())

    def z_finish(wide, field):
        @pl.when(has_up)
        def _():
            z_copy(wide, field, True).wait_send()
            z_copy(wide, field, False).wait_recv()

        @pl.when(has_down)
        def _():
            z_copy(wide, field, False).wait_send()
            z_copy(wide, field, True).wait_recv()

    def inside(x, y):
        return (x >= 0) & (x < n_gx) & (y >= 0) & (y < n_gy)

    def near_copy(wide, field, at, dx, dy, x, y):
        if dy == 0:
            src = wide.at[:, pl.ds(EDGE if dx < 0 else rows, EDGE), own]
            dst = wide.at[:, pl.ds(EDGE + rows if dx < 0 else 0, EDGE), own]
        else:
            side = 0 if dy > 0 else 1
            source, target, count = {
                0: (0, EDGE, rows), -1: (0, EDGE + rows, EDGE), 1: (rows - EDGE, 0, EDGE)
            }[dx]
            src = pack.at[field, pl.ds(source, count)]
            dst = sides.at[field, side, pl.ds(target, count)]
        return pltpu.make_async_remote_copy(
            src_ref=src, dst_ref=dst, send_sem=near_send.at[field, at], recv_sem=near_recv.at[field, at],
            device_id={"gx": x, "gy": y}, device_id_type=MESH,
        )

    def near_start(wide, field, faces):
        for at, (dx, dy) in enumerate(STEPS):
            if (dy == 0) != faces:
                continue

            @pl.when(inside(ix + dx, iy + dy))
            def _():
                near_copy(wide, field, at, dx, dy, ix + dx, iy + dy).start()

    def near_finish(wide, field):
        for at, (dx, dy) in enumerate(STEPS):
            @pl.when(inside(ix - dx, iy - dy))
            def _():
                near_copy(wide, field, at, dx, dy, ix - dx, iy - dy).wait_recv()

            @pl.when(inside(ix + dx, iy + dy))
            def _():
                near_copy(wide, field, at, dx, dy, ix + dx, iy + dy).wait_send()

    def unpack(wide, field):
        for i in range(nz + 4):
            wide[i, :, pl.ds(cols, cols)] = halo_columns(sides[field, 0], sides[field, 1], i, 4)

    loads[0].wait()
    z_start(wide_d, 0)

    depth = nz * 32
    place_row = lax.broadcasted_iota(jnp.int32, (span * nz, depth), 0)
    place_lane = lax.broadcasted_iota(jnp.int32, (span * nz, depth), 1)
    place = place_lane == lax.rem(place_row, nz) * 32 + place_row // nz
    place = jnp.where(place, 1.0, 0.0).astype(jnp.bfloat16)
    loads[6].wait()
    for c in range(comps):
        footprint = taps_ref[c].astype(jnp.float32).reshape(span * nz, span).astype(jnp.bfloat16)
        lines = lax.dot_general(
            footprint, place, (((0,), (0,)), ((), ())), preferred_element_type=jnp.float32
        )
        for b in range(span):
            first = (b * comps + c) * 16
            for half in range(depth // 128):
                taps = jnp.broadcast_to(lines[b : b + 1, half * 128 : (half + 1) * 128], (16, 128))
                band = pltpu.roll(taps, 0, 1, stride=1, stride_axis=0)
                toeplitz[first : first + 16, half * 128 : (half + 1) * 128] = band.astype(jnp.bfloat16)

    z_finish(wide_d, 0)
    near_start(wide_d, 0, True)
    pack[0] = packed_columns([wide_d[i, inner, own] for i in range(nz + 4)], 4)
    near_start(wide_d, 0, False)

    def landed(off):
        tile = lax.rem(me + off, tiles)
        copy = block_copy(tile, tile)
        copy.wait_recv()

    loads[1].wait()
    over_tiles(landed)
    slots = tiles * 16
    values = arrived[:, 0:16, :].reshape(slots, cols)
    picks = arrived[:, 16:32, :].reshape(slots, 128).astype(jnp.float32).T
    slot_z = lax.rem(lax.broadcasted_iota(jnp.int32, (128, slots), 1), nz)
    row_z = lax.broadcasted_iota(jnp.int32, (128, slots), 0) // rows
    for g in range(nz // 2):
        chosen = jnp.where(slot_z == row_z + 2 * g, picks, 0.0).astype(jnp.bfloat16)
        total = jnp.dot(chosen, values, preferred_element_type=jnp.float32)
        for j in range(2):
            trial = sigma_in[2 * g + j] - 0.5 * total[j * rows : (j + 1) * rows]
            wide_s[2 * g + j + 2, inner, own] = trial
            sigma_out[2 * g + j] = trial
    z_start(wide_s, 1)
    near_finish(wide_d, 0)
    unpack(wide_d, 0)
    z_finish(wide_s, 1)
    near_start(wide_s, 1, True)
    pack[1] = packed_columns([wide_s[i, inner, own] for i in range(nz + 4)], 4)
    near_start(wide_s, 1, False)
    near_finish(wide_s, 1)
    unpack(wide_s, 1)

    at_row = lax.broadcasted_iota(jnp.int32, (ext, 2 * cols), 0)
    at_lane = lax.broadcasted_iota(jnp.int32, (ext, 2 * cols), 1)
    row_in = ((at_row >= EDGE) | (ix > 0)) & ((at_row < EDGE + rows) | (ix < n_gx - 1))
    lane_in = (at_lane < cols) | ((at_lane < cols + 64) & (iy < n_gy - 1)) | ((at_lane >= cols + 64) & (iy > 0))

    def shifted(value, axis):
        size = value.shape[axis]
        return pltpu.roll(value, size - 1, axis) - pltpu.roll(value, 1, axis)

    for i in range(1, nz + 3):
        def gradient(wide):
            here = wide[i]
            return shifted(here, 0) * 0.5, shifted(here, 1) * 0.5, (wide[i + 1] - wide[i - 1]) * 0.5

        dx, dy, dz = gradient(wide_d)
        sx, sy, sz = gradient(wide_s)
        cx, cy, cz = dy * sz - dz * sy, dz * sx - dx * sz, dx * sy - dy * sx
        fz = sx * cy - sy * cx
        fz = fz[EDGE : EDGE + rows, :cols]
        if i == 1:
            fz = jnp.where(has_down, fz, 0.0)
        if i == nz + 2:
            fz = jnp.where(has_up, fz, 0.0)
        flux_z[i] = fz
        if 2 <= i < nz + 2:
            fx = jnp.where(row_in, sy * cz - sz * cy, 0.0)
            fy = jnp.where(lane_in, sz * cx - sx * cz, 0.0)
            lateral[i] = (shifted(fx, 0) + shifted(fy, 1))[EDGE : EDGE + rows, :cols]

    for i in range(nz):
        trial = wide_d[i + 2, inner, own] + 0.25 * (lateral[i + 2] + (flux_z[i + 3] - flux_z[i + 1]))
        density_out[i] = trial
        rounded[i, inner, own] = trial.astype(jnp.bfloat16).astype(jnp.float32)
    near_start(rounded, 2, True)
    pack[2] = packed_columns([rounded[i, inner, own] for i in range(nz)], 8)
    near_start(rounded, 2, False)
    near_finish(rounded, 2)
    for i in range(nz):
        rounded[i, :, pl.ds(cols, cols)] = halo_columns(sides[2, 0], sides[2, 1], i, 8)

    for s in range(rows // 16):
        for i in range(nz):
            blocks[s, i * 32 : (i + 1) * 32, :] = rounded[i, s * 16 : s * 16 + 32, :].astype(jnp.bfloat16)

    def swap(s):
        return pltpu.make_async_remote_copy(
            src_ref=part.at[:, pl.ds(s * 16, 16), :], dst_ref=other.at[:, pl.ds(s * 16, 16), :],
            send_sem=sum_send.at[s], recv_sem=sum_recv.at[s],
            device_id={"gz": n_gz - 1 - iz}, device_id_type=MESH,
        )

    for s in range(rows // 16):
        block = blocks[s]
        total = jnp.zeros((comps * 16, cols), jnp.float32)
        for b in range(span):
            one = jnp.dot(
                toeplitz[b * comps * 16 : (b + 1) * comps * 16, :], block, preferred_element_type=jnp.float32
            )
            total = total + pltpu.roll(one, (8 - b) % (2 * cols), 1)[:, :cols]
        for c in range(comps):
            part[c, s * 16 : (s + 1) * 16, :] = total[c * 16 : (c + 1) * 16]
        if n_gz > 1:
            swap(s).start()

    loads[2].wait()
    over_tiles(lambda off: block_copy(lax.rem(me + off, tiles), me).wait_send())
    for s in range(rows // 16):
        here = pl.ds(s * 16, 16)
        if n_gz > 1:
            swap(s).wait()
            residual_out[:, here, :] = part[:, here, :] + other[:, here, :] - observed_in[:, here, :]
        else:
            residual_out[:, here, :] = part[:, here, :] - observed_in[:, here, :]


def local(sizes, density, sigma, mt_values, mt_rows, mt_counts, kernel, observed):
    nz, rows, cols = density.shape
    tiles, capacity = mt_values.shape[1:3]
    comps, span = kernel.shape[0], kernel.shape[2]
    ext = rows + 2 * EDGE
    blocks = mt_values[0].reshape(tiles, capacity * nz, cols)
    taps = kernel.transpose(0, 2, 1, 3)
    vmem = pl.BlockSpec(memory_space=pltpu.VMEM)
    whole = pl.BlockSpec(memory_space=pltpu.HBM)
    f32 = jnp.float32
    dma = pltpu.SemaphoreType.DMA
    shapes = tuple(jax.ShapeDtypeStruct(like.shape, f32) for like in (sigma, density, observed))
    return pl.pallas_call(
        functools.partial(body, sizes),
        out_shape=shapes,
        in_specs=[whole] * 7,
        out_specs=(vmem,) * 3,
        scratch_shapes=[
            pltpu.VMEM(sigma.shape, f32),
            pltpu.VMEM(observed.shape, f32),
            pltpu.VMEM(blocks.shape, jnp.bfloat16),
            pltpu.SMEM((capacity, tiles), jnp.int32),
            pltpu.SMEM((1, tiles), jnp.int32),
            pltpu.VMEM(taps.shape, jnp.bfloat16),
            pltpu.VMEM((tiles, 32, 128), jnp.bfloat16),
            pltpu.VMEM((tiles, 32, 128), jnp.bfloat16),
            pltpu.VMEM((nz + 4, ext, 2 * cols), f32),
            pltpu.VMEM((nz + 4, ext, 2 * cols), f32),
            pltpu.VMEM((3, rows, 128), f32),
            pltpu.VMEM((3, 2, ext, 128), f32),
            pltpu.VMEM((nz + 4, rows, cols), f32),
            pltpu.VMEM((nz + 4, rows, cols), f32),
            pltpu.VMEM((nz, ext, 2 * cols), f32),
            pltpu.VMEM((span * comps * 16, nz * 32), jnp.bfloat16),
            pltpu.VMEM((rows // 16, nz * 32, 2 * cols), jnp.bfloat16),
            pltpu.VMEM(observed.shape, f32),
            pltpu.VMEM(observed.shape, f32),
            dma((7,)), dma((tiles,)), dma((tiles,)), dma((2, 2)), dma((2, 2)),
            dma((3, 8)), dma((3, 8)), dma((rows // 16,)), dma((rows // 16,)),
        ],
        compiler_params=pltpu.CompilerParams(
            collective_id=0, has_side_effects=True, vmem_limit_bytes=57 * 1024 * 1024
        ),
    )(density, sigma, blocks, mt_rows[0].T, mt_counts, taps, observed)


def solution(mesh):
    field = P(("grp", "gz"), "gx", "gy")
    placed = (
        field,
        field,
        P(("grp", "gx", "gy"), None, None, "gz", None),
        P(("grp", "gx", "gy"), None, None),
        P(("grp", "gx", "gy"), None),
        P(None, "gz", None, None),
        P("grp", "gx", "gy"),
    )
    sizes = (mesh.shape["gx"], mesh.shape["gy"], mesh.shape["gz"])
    return jax.shard_map(
        functools.partial(local, sizes),
        mesh=mesh,
        in_specs=placed,
        out_specs=(field, field, P("grp", "gx", "gy")),
        check_vma=False,
    )
```

```python
import functools

import jax
import jax.numpy as jnp
from jax import lax
from jax.experimental import pallas as pl
from jax.experimental.pallas import tpu as pltpu
from jax.sharding import PartitionSpec as P

MESH = pl.DeviceIdType.MESH
STEPS = ((-1, 0), (1, 0), (0, -1), (0, 1), (-1, -1), (-1, 1), (1, -1), (1, 1))
EDGE = 8


def packed_columns(layers, half):
    lane = lax.broadcasted_iota(jnp.int32, layers[0].shape, 1)
    result = jnp.zeros_like(layers[0])
    for i, layer in enumerate(layers):
        result = jnp.where(lane // (2 * half) == i, pltpu.roll(layer, half + 2 * half * i, 1), result)
    return result


def halo_columns(left, right, i, half):
    lane = lax.broadcasted_iota(jnp.int32, left.shape, 1)
    own = 2 * half * i
    return jnp.where(
        lane < 64,
        pltpu.roll(right, (128 - own - half) % 128, 1),
        pltpu.roll(left, (128 - half - own) % 128, 1),
    )


def body(
    sizes, density_ref, sigma_ref, values_in, rows_in, counts_in, taps_in, observed_ref,
    sigma_hbm, density_hbm, residual_out,
    sigma_out, density_out, sigma_in, observed_in, values_ref, rows_ref, counts_ref, taps_ref, payload, arrived, wide_d, wide_s, pack, sides, flux_z, lateral, rounded, toeplitz, blocks, part, other,
    load_sem, all_send, all_recv, z_send, z_recv, near_send, near_recv, sum_send, sum_recv,
):
    n_gx, n_gy, n_gz = sizes
    tiles = n_gx * n_gy
    nz, rows, cols = density_ref.shape
    comps = observed_ref.shape[0]
    span = taps_ref.shape[1]
    ext = rows + 2 * EDGE
    ix, iy, iz = lax.axis_index("gx"), lax.axis_index("gy"), lax.axis_index("gz")
    me = ix * n_gy + iy
    inner = pl.ds(EDGE, rows)
    own = pl.ds(0, cols)

    def over_tiles(step):
        if tiles <= 16:
            for off in range(1, tiles):
                step(off)
        else:
            lax.fori_loop(1, tiles, lambda off, _: (step(off), 0)[1], 0)

    loads = [
        pltpu.make_async_copy(density_ref, wide_d.at[pl.ds(2, nz), inner, own], load_sem.at[0]),
        pltpu.make_async_copy(sigma_ref, sigma_in, load_sem.at[1]),
        pltpu.make_async_copy(observed_ref, observed_in, load_sem.at[2]),
        pltpu.make_async_copy(values_in, values_ref, load_sem.at[3]),
        pltpu.make_async_copy(rows_in, rows_ref, load_sem.at[4]),
        pltpu.make_async_copy(counts_in, counts_ref, load_sem.at[5]),
        pltpu.make_async_copy(taps_in, taps_ref, load_sem.at[6]),
    ]
    for load in loads[3:] + loads[:3]:
        load.start()
    for wide in (wide_d, wide_s, rounded):
        depth = wide.shape[0]
        for first in (0, EDGE + rows):
            wide[:, first : first + EDGE, :cols] = jnp.zeros((depth, EDGE, cols), jnp.float32)
    for wide in (wide_d, wide_s):
        for first in (0, nz + 2):
            wide[first : first + 2, inner, own] = jnp.zeros((2, rows, cols), jnp.float32)
    sides[...] = jnp.zeros_like(sides)

    barrier = pltpu.get_barrier_semaphore()

    def greet(off):
        tile = lax.rem(me + off, tiles)
        pl.semaphore_signal(
            barrier, inc=1, device_id={"gx": tile // n_gy, "gy": lax.rem(tile, n_gy)}, device_id_type=MESH
        )

    over_tiles(greet)
    for off in range(1, n_gz):
        pl.semaphore_signal(barrier, inc=1, device_id={"gz": lax.rem(iz + off, n_gz)}, device_id_type=MESH)

    slot_row = lax.rem(lax.broadcasted_iota(jnp.int32, (nz, 128), 1), rows)

    def load_blocks(tile):
        payload[tile, 0:16, :] = values_ref[tile]
        picked = []
        for k in range(16 // nz):
            target = jnp.where(k < counts_ref[0, tile], rows_ref[k, tile], -1)
            picked.append(jnp.where(slot_row == target, 1.0, 0.0))
        payload[tile, 16:32, :] = jnp.concatenate(picked, axis=0).astype(jnp.bfloat16)

    for load in loads[3:6]:
        load.wait()
    if tiles <= 16:
        for tile in range(tiles):
            load_blocks(tile)
    else:
        lax.fori_loop(0, tiles, lambda tile, _: (load_blocks(tile), 0)[1], 0)
    pl.semaphore_wait(barrier, tiles - 1 + n_gz - 1)

    def block_copy(tile, source):
        return pltpu.make_async_remote_copy(
            src_ref=payload.at[tile], dst_ref=arrived.at[source],
            send_sem=all_send.at[tile], recv_sem=all_recv.at[source],
            device_id={"gx": tile // n_gy, "gy": lax.rem(tile, n_gy)}, device_id_type=MESH,
        )

    over_tiles(lambda off: block_copy(lax.rem(me + off, tiles), me).start())
    arrived[me] = payload[me]

    def z_copy(wide, field, up):
        src, dst = (pl.ds(nz, 2), pl.ds(0, 2)) if up else (pl.ds(2, 2), pl.ds(nz + 2, 2))
        return pltpu.make_async_remote_copy(
            src_ref=wide.at[src, inner, own], dst_ref=wide.at[dst, inner, own],
            send_sem=z_send.at[field, int(up)], recv_sem=z_recv.at[field, int(up)],
            device_id={"gz": lax.rem(iz + (1 if up else n_gz - 1), n_gz)}, device_id_type=MESH,
        )

    has_up, has_down = iz < n_gz - 1, iz > 0

    def z_start(wide, field):
        pl.when(has_up)(lambda: z_copy(wide, field, True).start())
        pl.when(has_down)(lambda: z_copy(wide, field, False).start())

    def z_finish(wide, field):
        @pl.when(has_up)
        def _():
            z_copy(wide, field, True).wait_send()
            z_copy(wide, field, False).wait_recv()

        @pl.when(has_down)
        def _():
            z_copy(wide, field, False).wait_send()
            z_copy(wide, field, True).wait_recv()

    def inside(x, y):
        return (x >= 0) & (x < n_gx) & (y >= 0) & (y < n_gy)

    def near_copy(wide, field, at, dx, dy, x, y):
        if dy == 0:
            src = wide.at[:, pl.ds(EDGE if dx < 0 else rows, EDGE), own]
            dst = wide.at[:, pl.ds(EDGE + rows if dx < 0 else 0, EDGE), own]
        else:
            side = 0 if dy > 0 else 1
            source, target, count = {
                0: (0, EDGE, rows), -1: (0, EDGE + rows, EDGE), 1: (rows - EDGE, 0, EDGE)
            }[dx]
            src = pack.at[field, pl.ds(source, count)]
            dst = sides.at[field, side, pl.ds(target, count)]
        return pltpu.make_async_remote_copy(
            src_ref=src, dst_ref=dst, send_sem=near_send.at[field, at], recv_sem=near_recv.at[field, at],
            device_id={"gx": x, "gy": y}, device_id_type=MESH,
        )

    def near_start(wide, field, faces):
        for at, (dx, dy) in enumerate(STEPS):
            if (dy == 0) != faces:
                continue

            @pl.when(inside(ix + dx, iy + dy))
            def _():
                near_copy(wide, field, at, dx, dy, ix + dx, iy + dy).start()

    def near_finish(wide, field):
        for at, (dx, dy) in enumerate(STEPS):
            @pl.when(inside(ix - dx, iy - dy))
            def _():
                near_copy(wide, field, at, dx, dy, ix - dx, iy - dy).wait_recv()

            @pl.when(inside(ix + dx, iy + dy))
            def _():
                near_copy(wide, field, at, dx, dy, ix + dx, iy + dy).wait_send()

    def unpack(wide, field):
        for i in range(nz + 4):
            wide[i, :, pl.ds(cols, cols)] = halo_columns(sides[field, 0], sides[field, 1], i, 4)

    loads[0].wait()
    z_start(wide_d, 0)

    depth = nz * 32
    place_row = lax.broadcasted_iota(jnp.int32, (span * nz, depth), 0)
    place_lane = lax.broadcasted_iota(jnp.int32, (span * nz, depth), 1)
    place = place_lane == lax.rem(place_row, nz) * 32 + place_row // nz
    place = jnp.where(place, 1.0, 0.0).astype(jnp.bfloat16)
    loads[6].wait()
    for c in range(comps):
        footprint = taps_ref[c].astype(jnp.float32).reshape(span * nz, span).astype(jnp.bfloat16)
        lines = lax.dot_general(
            footprint, place, (((0,), (0,)), ((), ())), preferred_element_type=jnp.float32
        )
        for b in range(span):
            first = (b * comps + c) * 16
            for half in range(depth // 128):
                taps = jnp.broadcast_to(lines[b : b + 1, half * 128 : (half + 1) * 128], (16, 128))
                band = pltpu.roll(taps, 0, 1, stride=1, stride_axis=0)
                toeplitz[first : first + 16, half * 128 : (half + 1) * 128] = band.astype(jnp.bfloat16)

    z_finish(wide_d, 0)
    near_start(wide_d, 0, True)
    pack[0] = packed_columns([wide_d[i, inner, own] for i in range(nz + 4)], 4)
    near_start(wide_d, 0, False)

    def landed(off):
        tile = lax.rem(me + off, tiles)
        copy = block_copy(tile, tile)
        copy.wait_recv()

    loads[1].wait()
    over_tiles(landed)
    slots = tiles * 16
    values = arrived[:, 0:16, :].reshape(slots, cols)
    picks = arrived[:, 16:32, :].reshape(slots, 128).astype(jnp.float32).T
    slot_z = lax.rem(lax.broadcasted_iota(jnp.int32, (128, slots), 1), nz)
    row_z = lax.broadcasted_iota(jnp.int32, (128, slots), 0) // rows
    for g in range(nz // 2):
        chosen = jnp.where(slot_z == row_z + 2 * g, picks, 0.0).astype(jnp.bfloat16)
        total = jnp.dot(chosen, values, preferred_element_type=jnp.float32)
        for j in range(2):
            trial = sigma_in[2 * g + j] - 0.5 * total[j * rows : (j + 1) * rows]
            wide_s[2 * g + j + 2, inner, own] = trial
            sigma_out[2 * g + j] = trial
    z_start(wide_s, 1)
    saves = [
        pltpu.make_async_copy(sigma_out, sigma_hbm, load_sem.at[7]),
        pltpu.make_async_copy(density_out, density_hbm, load_sem.at[8]),
    ]
    saves[0].start()
    near_finish(wide_d, 0)
    unpack(wide_d, 0)
    z_finish(wide_s, 1)
    near_start(wide_s, 1, True)
    pack[1] = packed_columns([wide_s[i, inner, own] for i in range(nz + 4)], 4)
    near_start(wide_s, 1, False)
    near_finish(wide_s, 1)
    unpack(wide_s, 1)

    at_row = lax.broadcasted_iota(jnp.int32, (ext, 2 * cols), 0)
    at_lane = lax.broadcasted_iota(jnp.int32, (ext, 2 * cols), 1)
    row_in = ((at_row >= EDGE) | (ix > 0)) & ((at_row < EDGE + rows) | (ix < n_gx - 1))
    lane_in = (at_lane < cols) | ((at_lane < cols + 64) & (iy < n_gy - 1)) | ((at_lane >= cols + 64) & (iy > 0))

    def shifted(value, axis):
        size = value.shape[axis]
        return pltpu.roll(value, size - 1, axis) - pltpu.roll(value, 1, axis)

    for i in range(1, nz + 3):
        def gradient(wide):
            here = wide[i]
            return shifted(here, 0) * 0.5, shifted(here, 1) * 0.5, (wide[i + 1] - wide[i - 1]) * 0.5

        dx, dy, dz = gradient(wide_d)
        sx, sy, sz = gradient(wide_s)
        cx, cy, cz = dy * sz - dz * sy, dz * sx - dx * sz, dx * sy - dy * sx
        fz = sx * cy - sy * cx
        fz = fz[EDGE : EDGE + rows, :cols]
        if i == 1:
            fz = jnp.where(has_down, fz, 0.0)
        if i == nz + 2:
            fz = jnp.where(has_up, fz, 0.0)
        flux_z[i] = fz
        if 2 <= i < nz + 2:
            fx = jnp.where(row_in, sy * cz - sz * cy, 0.0)
            fy = jnp.where(lane_in, sz * cx - sx * cz, 0.0)
            lateral[i] = (shifted(fx, 0) + shifted(fy, 1))[EDGE : EDGE + rows, :cols]

    for i in range(nz):
        trial = wide_d[i + 2, inner, own] + 0.25 * (lateral[i + 2] + (flux_z[i + 3] - flux_z[i + 1]))
        density_out[i] = trial
        rounded[i, inner, own] = trial.astype(jnp.bfloat16).astype(jnp.float32)
    near_start(rounded, 2, True)
    saves[1].start()
    pack[2] = packed_columns([rounded[i, inner, own] for i in range(nz)], 8)
    near_start(rounded, 2, False)
    near_finish(rounded, 2)
    for i in range(nz):
        rounded[i, :, pl.ds(cols, cols)] = halo_columns(sides[2, 0], sides[2, 1], i, 8)

    for s in range(rows // 16):
        for i in range(nz):
            blocks[s, i * 32 : (i + 1) * 32, :] = rounded[i, s * 16 : s * 16 + 32, :].astype(jnp.bfloat16)

    def swap(s):
        return pltpu.make_async_remote_copy(
            src_ref=part.at[:, pl.ds(s * 16, 16), :], dst_ref=other.at[:, pl.ds(s * 16, 16), :],
            send_sem=sum_send.at[s], recv_sem=sum_recv.at[s],
            device_id={"gz": n_gz - 1 - iz}, device_id_type=MESH,
        )

    for s in range(rows // 16):
        block = blocks[s]
        total = jnp.zeros((comps * 16, cols), jnp.float32)
        for b in range(span):
            one = jnp.dot(
                toeplitz[b * comps * 16 : (b + 1) * comps * 16, :], block, preferred_element_type=jnp.float32
            )
            total = total + pltpu.roll(one, (8 - b) % (2 * cols), 1)[:, :cols]
        for c in range(comps):
            part[c, s * 16 : (s + 1) * 16, :] = total[c * 16 : (c + 1) * 16]
        if n_gz > 1:
            swap(s).start()

    loads[2].wait()
    for save in saves:
        save.wait()
    over_tiles(lambda off: block_copy(lax.rem(me + off, tiles), me).wait_send())
    for s in range(rows // 16):
        here = pl.ds(s * 16, 16)
        if n_gz > 1:
            swap(s).wait()
            residual_out[:, here, :] = part[:, here, :] + other[:, here, :] - observed_in[:, here, :]
        else:
            residual_out[:, here, :] = part[:, here, :] - observed_in[:, here, :]


def local(sizes, density, sigma, mt_values, mt_rows, mt_counts, kernel, observed):
    nz, rows, cols = density.shape
    tiles, capacity = mt_values.shape[1:3]
    comps, span = kernel.shape[0], kernel.shape[2]
    ext = rows + 2 * EDGE
    blocks = mt_values[0].reshape(tiles, capacity * nz, cols)
    taps = kernel.transpose(0, 2, 1, 3)
    vmem = pl.BlockSpec(memory_space=pltpu.VMEM)
    whole = pl.BlockSpec(memory_space=pltpu.HBM)
    f32 = jnp.float32
    dma = pltpu.SemaphoreType.DMA
    shapes = tuple(jax.ShapeDtypeStruct(like.shape, f32) for like in (sigma, density, observed))
    return pl.pallas_call(
        functools.partial(body, sizes),
        out_shape=shapes,
        in_specs=[whole] * 7,
        out_specs=(whole, whole, vmem),
        scratch_shapes=[
            pltpu.VMEM(sigma.shape, f32),
            pltpu.VMEM(density.shape, f32),
            pltpu.VMEM(sigma.shape, f32),
            pltpu.VMEM(observed.shape, f32),
            pltpu.VMEM(blocks.shape, jnp.bfloat16),
            pltpu.SMEM((capacity, tiles), jnp.int32),
            pltpu.SMEM((1, tiles), jnp.int32),
            pltpu.VMEM(taps.shape, jnp.bfloat16),
            pltpu.VMEM((tiles, 32, 128), jnp.bfloat16),
            pltpu.VMEM((tiles, 32, 128), jnp.bfloat16),
            pltpu.VMEM((nz + 4, ext, 2 * cols), f32),
            pltpu.VMEM((nz + 4, ext, 2 * cols), f32),
            pltpu.VMEM((3, rows, 128), f32),
            pltpu.VMEM((3, 2, ext, 128), f32),
            pltpu.VMEM((nz + 4, rows, cols), f32),
            pltpu.VMEM((nz + 4, rows, cols), f32),
            pltpu.VMEM((nz, ext, 2 * cols), f32),
            pltpu.VMEM((span * comps * 16, nz * 32), jnp.bfloat16),
            pltpu.VMEM((rows // 16, nz * 32, 2 * cols), jnp.bfloat16),
            pltpu.VMEM(observed.shape, f32),
            pltpu.VMEM(observed.shape, f32),
            dma((9,)), dma((tiles,)), dma((tiles,)), dma((2, 2)), dma((2, 2)),
            dma((3, 8)), dma((3, 8)), dma((rows // 16,)), dma((rows // 16,)),
        ],
        compiler_params=pltpu.CompilerParams(
            collective_id=0, has_side_effects=True, vmem_limit_bytes=57 * 1024 * 1024
        ),
    )(density, sigma, blocks, mt_rows[0].T, mt_counts, taps, observed)


def solution(mesh):
    field = P(("grp", "gz"), "gx", "gy")
    placed = (
        field,
        field,
        P(("grp", "gx", "gy"), None, None, "gz", None),
        P(("grp", "gx", "gy"), None, None),
        P(("grp", "gx", "gy"), None),
        P(None, "gz", None, None),
        P("grp", "gx", "gy"),
    )
    sizes = (mesh.shape["gx"], mesh.shape["gy"], mesh.shape["gz"])
    return jax.shard_map(
        functools.partial(local, sizes),
        mesh=mesh,
        in_specs=placed,
        out_specs=(field, field, P("grp", "gx", "gy")),
        check_vma=False,
    )
```
